512 devices in a mesh: ka: 64 (over z, x, y_lo), ta: 8 (over y_hi, core).
Axes of the slice: x: 4, y: 8 (y_hi: 4, y_lo: 2; y = y_hi * 2 + y_lo), z: 8, core: 2. Of those that a mesh axis runs over, the one named last changes fastest.
Arguments:
- green_time: bfloat16 [2048, 256, 256], P(('ta', 'ka')), parts along dimension 0, may hold values from -0.375 to 0.375
- orbitals: bfloat16 [256, 256, 512], P('ka'), may hold values from -3.296875 to 3.296875
- pair_table: int32 [256, 256], P(None, 'ka'), may hold values from 0 to 255, as said below
- pair_momenta: int32 [2], replicated, may hold values from 0 to 255
- owner_rows: int32 [512], replicated, may hold values from 0 to 511, each once
Outputs:
- bubble: float32 [4096, 2, 512], P(('ta', 'ka')), parts along dimension 0
The draws below stay inside these ranges and needn't reach their ends.
There are 8 independent parts, one for each index of `ta`. The reference program is written for one: setup_inputs(seed, part) draws one part's arguments, and reference() takes and returns one part's arrays. A program takes and returns all parts, laid end to end along the dimension named above; an argument that names none is the same for every part. Nothing has to cross between parts.
Inputs may be any that keep to these rules, and one draw needn't show every extreme that they name: The momenta form a 4 x 4 x (16) periodic lattice listed in an order drawn from the seed; row a of pair_table gives, for each k, the index of momentum a minus momentum k, so every row is a permutation of 0 to 255.
All inputs are finite; a program needn't handle non-finite values.
Results may differ from the reference program's by a relative error of at most 0.0057.
Values may be sent and summed in bfloat16 or wider, within the bound.
A program may use at most 64 MiB of HBM per device.

```python
import jax
import jax.numpy as jnp

NORB = 256
NPTS = 512
NQ = 2
NK = 256


def draw_pair_table(key, part):
    lattice_order = jax.random.permutation(key, NK).astype(jnp.int32)
    extent_third = NK // 16
    comp_first = lattice_order // (4 * extent_third)
    comp_second = lattice_order // extent_third % 4
    comp_third = lattice_order % extent_third
    diff_first = (comp_first[:, None] - comp_first[None, :]) % 4
    diff_second = (comp_second[:, None] - comp_second[None, :]) % 4
    diff_third = (comp_third[:, None] - comp_third[None, :]) % extent_third
    lattice_points = (diff_first * 4 + diff_second) * extent_third + diff_third
    inverse_order = jnp.zeros((NK,), jnp.int32).at[lattice_order].set(jnp.arange(NK, dtype=jnp.int32))
    return jnp.take(inverse_order, lattice_points).astype(jnp.int32)


def block_levels(rng, dims, cuts, smallest, largest):
    loudness = 1.0
    for position, parts in cuts:
        heights = jax.random.uniform(jax.random.fold_in(jax.random.fold_in(rng, 6), position), (parts,), jnp.float32, smallest / len(cuts), largest / len(cuts))
        loudness = loudness * jnp.repeat(jnp.exp(heights), dims[position] // parts).reshape((-1,) + (1,) * (len(dims) - 1 - position))
    return loudness


def noise(key, dims, deviation, bound, pieces=(), held_as=jnp.bfloat16):
    entries = jax.random.normal(key, dims, jnp.float32) * deviation
    if len(pieces) > 0:
        entries = block_levels(key, dims, pieces, -0.22, 0.18) * entries
    return jnp.clip(entries, min=-bound, max=bound).astype(held_as)


def setup_inputs(seed: int = 0, part: int = 0) -> dict:
    splits = jax.random.split(jax.random.key(seed), 6)
    part_splits = jax.random.split(jax.random.fold_in(splits[5], part), 6)
    return {
        "green_time": noise(part_splits[0], (NK, NORB, NORB), NORB ** -0.5, 0.375, ((0, 64),)),
        "orbitals": noise(splits[1], (NK, NORB, NPTS), 0.55, 3.296875, ((0, 64),)),
        "pair_table": draw_pair_table(jax.random.fold_in(splits[5], 71), part),
        "pair_momenta": jax.random.randint(splits[3], (NQ,), 0, NK).astype(jnp.int32),
        "owner_rows": jax.random.permutation(splits[4], NPTS).astype(jnp.int32),
    }


def reference(green_time, orbitals, pair_table, pair_momenta, owner_rows):
    orbitals_owned = jnp.take(orbitals, owner_rows, axis=2)
    half_product = jnp.einsum("kij,kjp->kip", green_time.astype(jnp.float32), orbitals.astype(jnp.float32)).astype(jnp.bfloat16)
    projected = jnp.einsum("kia,kip->kap", orbitals_owned.astype(jnp.float32), half_product.astype(jnp.float32)).astype(jnp.bfloat16)
    partners = jnp.take(pair_table, pair_momenta, axis=0)
    widened = projected.astype(jnp.float32)
    per_pair = []
    for which in range(NQ):
        partner_blocks = jnp.take(widened, partners[which], axis=0)
        per_pair.append(jnp.sum(widened * partner_blocks, axis=0))
    return jnp.stack(per_pair, axis=1) * (1.0 / NK)
```

```python
import functools

import jax
import jax.numpy as jnp
from jax import lax
from jax.experimental import pallas as pl
from jax.experimental.pallas import tpu as pltpu
from jax.sharding import PartitionSpec as P

MESH = pl.DeviceIdType.MESH


def kernel(
    n, q_ref, green_ref, orb_ref, table_ref, owner_ref, out_ref,
    green, orb, select, owned, send, recv, pair_send, pair_recv, pairs,
    load_sem, send_sem, recv_sem, pair_send_sem, pair_recv_sem, local_sem,
):
    me = lax.axis_index("ka")
    per, norb, npts = green.shape[0], orb.shape[1], orb.shape[2]
    nq = q_ref.shape[0]
    rows = npts // n
    half = npts // 2

    load_green = pltpu.make_async_copy(green_ref, green, load_sem.at[0])
    load_orb = pltpu.make_async_copy(orb_ref, orb, load_sem.at[1])
    load_orb.start()
    load_green.start()

    barrier = pltpu.get_barrier_semaphore()

    @pl.loop(1, n)
    def _(step):
        peer = lax.rem(me + step, n)
        pl.semaphore_signal(barrier, inc=1, device_id={"ka": peer}, device_id_type=MESH)

    for q in range(nq):
        rows_of_table = lax.broadcasted_iota(jnp.int32, table_ref.shape, 0)
        chosen = jnp.where(rows_of_table == q_ref[q], table_ref[...], 0)
        pair_send[0, q : q + 1, 0:per] = jnp.sum(chosen, axis=0, keepdims=True)

    owner_columns = jnp.transpose(
        jnp.broadcast_to(owner_ref[...].astype(jnp.float32), (128, npts))
    )
    for tile in range(npts // 128):
        points = (lax.broadcasted_iota(jnp.int32, (npts, 128), 1) + tile * 128).astype(jnp.float32)
        select[:, tile * 128 : (tile + 1) * 128] = jnp.where(
            owner_columns == points, 1.0, 0.0
        ).astype(jnp.bfloat16)

    load_orb.wait()
    load_green.wait()
    for k in range(per):
        owned[...] = lax.dot_general(
            select[...], orb[k], (((1,), (1,)), ((), ())), preferred_element_type=jnp.float32
        ).astype(jnp.bfloat16)
        half_product = jnp.dot(
            green[k], orb[k], preferred_element_type=jnp.float32
        ).astype(jnp.bfloat16)
        projected = jnp.dot(owned[...], half_product, preferred_element_type=jnp.float32)
        projected = projected.reshape(n, rows, npts)
        send[:, k] = jnp.concatenate(
            [projected[:, :, :half], projected[:, :, half:]], axis=1
        ).astype(jnp.bfloat16)

    pl.semaphore_wait(barrier, n - 1)

    def block_copy(step):
        peer = lax.rem(me + step, n)
        return pltpu.make_async_remote_copy(
            src_ref=send.at[peer],
            dst_ref=recv.at[pl.ds(me * per, per)],
            send_sem=send_sem.at[step],
            recv_sem=recv_sem.at[step],
            device_id={"ka": peer},
            device_id_type=MESH,
        )

    def pair_copy(step):
        peer = lax.rem(me + step, n)
        return pltpu.make_async_remote_copy(
            src_ref=pair_send.at[0],
            dst_ref=pair_recv.at[me],
            send_sem=pair_send_sem.at[step],
            recv_sem=pair_recv_sem.at[step],
            device_id={"ka": peer},
            device_id_type=MESH,
        )

    @pl.loop(1, n)
    def _(step):
        pair_copy(step).start()

    @pl.loop(1, n)
    def _(step):
        block_copy(step).start()

    own = pltpu.make_async_copy(send.at[me], recv.at[pl.ds(me * per, per)], local_sem.at[0])
    own.start()
    own_pair = pltpu.make_async_copy(pair_send.at[0], pair_recv.at[me], local_sem.at[1])
    own_pair.start()
    own.wait()
    own_pair.wait()

    @pl.loop(1, n)
    def _(step):
        pair_copy(step).wait()

    to_scalar = pltpu.make_async_copy(pair_recv, pairs, local_sem.at[2])
    to_scalar.start()
    to_scalar.wait()

    @pl.loop(1, n)
    def _(step):
        block_copy(step).wait()

    def add(device, totals):
        totals = list(totals)
        for j in range(per):
            mine = recv[device * per + j].astype(jnp.float32)
            for q in range(nq):
                partner = recv[pairs[device, q, j]].astype(jnp.float32)
                totals[q] = totals[q] + mine * partner
        return tuple(totals)

    zero = jnp.zeros(recv.shape[1:], jnp.float32)
    totals = lax.fori_loop(0, n, add, (zero,) * nq)
    for q in range(nq):
        scaled = totals[q] * (1.0 / (n * per))
        out_ref[:, q * npts : q * npts + half] = scaled[:rows]
        out_ref[:, q * npts + half : (q + 1) * npts] = scaled[rows:]


def solution(mesh):
    n = mesh.shape["ka"]

    def per_device(green_time, orbitals, pair_table, pair_momenta, owner_rows):
        per, norb, npts = orbitals.shape
        nq = pair_momenta.shape[0]
        rows = npts // n
        bf16, i32 = jnp.bfloat16, jnp.int32
        out = pl.pallas_call(
            functools.partial(kernel, n),
            out_shape=jax.ShapeDtypeStruct((rows, nq * npts), jnp.float32),
            in_specs=[
                pl.BlockSpec(memory_space=pltpu.SMEM),
                pl.BlockSpec(memory_space=pl.ANY),
                pl.BlockSpec(memory_space=pl.ANY),
                pl.BlockSpec(memory_space=pltpu.VMEM),
                pl.BlockSpec(memory_space=pltpu.VMEM),
            ],
            out_specs=pl.BlockSpec(memory_space=pltpu.VMEM),
            scratch_shapes=[
                pltpu.VMEM((per, norb, norb), bf16),
                pltpu.VMEM((per, norb, npts), bf16),
                pltpu.VMEM((npts, npts), bf16),
                pltpu.VMEM((npts, norb), bf16),
                pltpu.VMEM((n, per, 2 * rows, npts // 2), bf16),
                pltpu.VMEM((n * per, 2 * rows, npts // 2), bf16),
                pltpu.VMEM((1, nq, 128), i32),
                pltpu.VMEM((n, nq, 128), i32),
                pltpu.SMEM((n, nq, 128), i32),
                pltpu.SemaphoreType.DMA((2,)),
                pltpu.SemaphoreType.DMA((n,)),
                pltpu.SemaphoreType.DMA((n,)),
                pltpu.SemaphoreType.DMA((n,)),
                pltpu.SemaphoreType.DMA((n,)),
                pltpu.SemaphoreType.DMA((3,)),
            ],
            compiler_params=pltpu.CompilerParams(
                collective_id=0, has_side_effects=True, vmem_limit_bytes=32 * 1024 * 1024
            ),
            cost_estimate=pl.CostEstimate(
                flops=2 * per * npts * (norb * norb + npts * norb * 2),
                bytes_accessed=2 * per * norb * (norb + npts),
                transcendentals=0,
            ),
        )(pair_momenta, green_time, orbitals, pair_table, owner_rows.reshape(1, npts))
        return out.reshape(rows, nq, npts)

    return jax.shard_map(
        per_device,
        mesh=mesh,
        in_specs=(P(("ta", "ka"), None, None), P("ka", None, None), P(None, "ka"), P(), P()),
        out_specs=P(("ta", "ka"), None, None),
        check_vma=False,
    )
```

```python
import functools

import jax
import jax.numpy as jnp
from jax import lax
from jax.experimental import pallas as pl
from jax.experimental.pallas import tpu as pltpu
from jax.sharding import PartitionSpec as P

MESH = pl.DeviceIdType.MESH
PLANE = 8
LANES = 128


def kernel(
    n, q_hbm, green_hbm, orb_hbm, table_hbm, owner_hbm, out_ref,
    q_ref, green, orb, table, owner, select, owned, send, recv,
    plane_send, plane_recv, line_send, line_recv, pairs,
    load_sem, send_sem, recv_sem, plane_send_sem, plane_recv_sem, line_send_sem, line_recv_sem, local_sem,
):
    me = lax.axis_index("ka")
    line, spot = me // PLANE, me % PLANE
    lines = n // PLANE
    per, norb, npts = orb.shape
    nq = q_ref.shape[0]
    rows = npts // n
    half = npts // 2

    barrier = pltpu.get_barrier_semaphore()

    @pl.loop(1, n)
    def _(step):
        peer = lax.rem(me + step, n)
        pl.semaphore_signal(barrier, inc=1, device_id={"ka": peer}, device_id_type=MESH)

    loads = [
        pltpu.make_async_copy(source, held, load_sem.at[i])
        for i, (source, held) in enumerate(
            ((owner_hbm, owner), (q_hbm, q_ref), (table_hbm, table), (orb_hbm, orb), (green_hbm, green))
        )
    ]
    for load in loads:
        load.start()
    for load in loads[:3]:
        load.wait()

    owner_columns = jnp.transpose(
        jnp.broadcast_to(owner[...].astype(jnp.float32), (LANES, npts))
    )
    for tile in range(npts // LANES):
        points = lax.broadcasted_iota(jnp.int32, (npts, LANES), 1) + tile * LANES
        select[:, tile * LANES : (tile + 1) * LANES] = jnp.where(
            owner_columns == points.astype(jnp.float32), 1.0, 0.0
        ).astype(jnp.bfloat16)

    table_columns = lax.broadcasted_iota(jnp.int32, table.shape, 1)
    lane = lax.broadcasted_iota(jnp.int32, (per, LANES), 1)
    which = lax.broadcasted_iota(jnp.int32, (per, LANES), 0)
    placed = jnp.zeros((per, LANES), jnp.int32)
    for q in range(nq):
        chosen = jnp.where(table_columns == q_ref[q], table[...], 0)
        partner = jnp.sum(chosen, axis=1, keepdims=True)
        placed += jnp.where(lane == (spot * nq + q) * per + which, partner, 0)
    plane_send[0] = jnp.sum(placed, axis=0, keepdims=True)

    for load in loads[3:]:
        load.wait()
    for k in range(per):
        owned[...] = lax.dot_general(
            select[...], orb[k], (((1,), (1,)), ((), ())), preferred_element_type=jnp.float32
        ).astype(jnp.bfloat16)
        half_product = jnp.dot(
            green[k], orb[k], preferred_element_type=jnp.float32
        ).astype(jnp.bfloat16)
        projected = jnp.dot(owned[...], half_product, preferred_element_type=jnp.float32)
        projected = projected.reshape(n, rows, npts)
        send[:, k] = jnp.concatenate(
            [projected[:, :, :half], projected[:, :, half:]], axis=1
        ).astype(jnp.bfloat16)

    pl.semaphore_wait(barrier, n - 1)

    def block_copy(step):
        peer = lax.rem(line + step % lines, lines) * PLANE + lax.rem(spot + step // lines, PLANE)
        return pltpu.make_async_remote_copy(
            src_ref=send.at[peer],
            dst_ref=recv.at[pl.ds(me * per, per)],
            send_sem=send_sem.at[step],
            recv_sem=recv_sem.at[step],
            device_id={"ka": peer},
            device_id_type=MESH,
        )

    def plane_copy(step):
        return pltpu.make_async_remote_copy(
            src_ref=plane_send.at[0],
            dst_ref=plane_recv.at[spot],
            send_sem=plane_send_sem.at[step],
            recv_sem=plane_recv_sem.at[step],
            device_id={"ka": line * PLANE + lax.rem(spot + step, PLANE)},
            device_id_type=MESH,
        )

    def line_copy(step):
        return pltpu.make_async_remote_copy(
            src_ref=line_send.at[0],
            dst_ref=line_recv.at[line],
            send_sem=line_send_sem.at[step],
            recv_sem=line_recv_sem.at[step],
            device_id={"ka": lax.rem(line + step, lines) * PLANE + spot},
            device_id_type=MESH,
        )

    @pl.loop(1, PLANE)
    def _(step):
        plane_copy(step).start()

    @pl.loop(1, n // 2)
    def _(step):
        block_copy(step).start()

    own = pltpu.make_async_copy(send.at[me], recv.at[pl.ds(me * per, per)], local_sem.at[0])
    own.start()
    plane_own = pltpu.make_async_copy(plane_send.at[0], plane_recv.at[spot], local_sem.at[1])
    plane_own.start()
    plane_own.wait()

    @pl.loop(1, PLANE)
    def _(step):
        plane_copy(step).wait()

    line_send[0] = jnp.sum(plane_recv[...], axis=0)

    @pl.loop(1, lines)
    def _(step):
        line_copy(step).start()

    line_own = pltpu.make_async_copy(line_send.at[0], line_recv.at[line], local_sem.at[2])
    line_own.start()

    @pl.loop(n // 2, n)
    def _(step):
        block_copy(step).start()

    own.wait()
    line_own.wait()

    @pl.loop(1, lines)
    def _(step):
        line_copy(step).wait()

    to_scalar = pltpu.make_async_copy(line_recv, pairs, local_sem.at[3])
    to_scalar.start()
    to_scalar.wait()

    @pl.loop(1, n)
    def _(step):
        block_copy(step).wait()

    def add(device, totals):
        totals = list(totals)
        for j in range(per):
            mine = recv[device * per + j].astype(jnp.float32)
            for q in range(nq):
                at = pairs[device // PLANE, 0, (device % PLANE * nq + q) * per + j]
                totals[q] = totals[q] + mine * recv[at].astype(jnp.float32)
        return tuple(totals)

    zero = jnp.zeros(recv.shape[1:], jnp.float32)
    totals = lax.fori_loop(0, n, add, (zero,) * nq, unroll=4)
    for q in range(nq):
        scaled = totals[q] * (1.0 / (n * per))
        out_ref[:, q * npts : q * npts + half] = scaled[:rows]
        out_ref[:, q * npts + half : (q + 1) * npts] = scaled[rows:]


def solution(mesh):
    n = mesh.shape["ka"]

    def per_device(green_time, orbitals, pair_table, pair_momenta, owner_rows):
        per, norb, npts = orbitals.shape
        nq = pair_momenta.shape[0]
        rows = npts // n
        bf16, i32 = jnp.bfloat16, jnp.int32
        dma = pltpu.SemaphoreType.DMA
        out = pl.pallas_call(
            functools.partial(kernel, n),
            out_shape=jax.ShapeDtypeStruct((rows, nq * npts), jnp.float32),
            in_specs=[pl.BlockSpec(memory_space=pltpu.HBM)] * 5,
            out_specs=pl.BlockSpec(memory_space=pltpu.VMEM),
            scratch_shapes=[
                pltpu.SMEM((nq,), i32),
                pltpu.VMEM((per, norb, norb), bf16),
                pltpu.VMEM((per, norb, npts), bf16),
                pltpu.VMEM((per, n * per), i32),
                pltpu.VMEM((1, npts), i32),
                pltpu.VMEM((npts, npts), bf16),
                pltpu.VMEM((npts, norb), bf16),
                pltpu.VMEM((n, per, 2 * rows, npts // 2), bf16),
                pltpu.VMEM((n * per, 2 * rows, npts // 2), bf16),
                pltpu.VMEM((1, 1, LANES), i32),
                pltpu.VMEM((PLANE, 1, LANES), i32),
                pltpu.VMEM((1, 1, LANES), i32),
                pltpu.VMEM((n // PLANE, 1, LANES), i32),
                pltpu.SMEM((n // PLANE, 1, LANES), i32),
                dma((5,)),
                dma((n,)),
                dma((n,)),
                dma((PLANE,)),
                dma((PLANE,)),
                dma((n // PLANE,)),
                dma((n // PLANE,)),
                dma((4,)),
            ],
            compiler_params=pltpu.CompilerParams(
                collective_id=0, has_side_effects=True, vmem_limit_bytes=56 * 1024 * 1024
            ),
            cost_estimate=pl.CostEstimate(
                flops=2 * per * npts * (norb * norb + npts * norb * 2),
                bytes_accessed=2 * per * norb * (norb + npts),
                transcendentals=0,
            ),
        )(pair_momenta, green_time, orbitals, pair_table.T, owner_rows.reshape(1, npts))
        return out.reshape(rows, nq, npts)

    return jax.shard_map(
        per_device,
        mesh=mesh,
        in_specs=(P(("ta", "ka"), None, None), P("ka", None, None), P(None, "ka"), P(), P()),
        out_specs=P(("ta", "ka"), None, None),
        check_vma=False,
    )
```

```python
import functools

import jax
import jax.numpy as jnp
from jax import lax
from jax.experimental import pallas as pl
from jax.experimental.pallas import tpu as pltpu
from jax.sharding import PartitionSpec as P

MESH = pl.DeviceIdType.MESH
PLANE = 8
LANES = 128


def kernel(
    n, q_hbm, green_hbm, orb_hbm, table_hbm, owner_hbm, out_ref,
    q_ref, green, orb, table, owner, select, owned, send, recv,
    plane_send, plane_recv, line_send, line_recv, pairs,
    load_sem, send_sem, recv_sem, plane_send_sem, plane_recv_sem, line_send_sem, line_recv_sem, local_sem, ready_sem,
):
    me = lax.axis_index("ka")
    line, spot = me // PLANE, me % PLANE
    lines = n // PLANE
    per, norb, npts = orb.shape
    nq = q_ref.shape[0]
    rows = npts // n
    half = npts // 2

    def in_plane(step):
        return {"ka": line * PLANE + lax.rem(spot + step, PLANE)}

    def in_line(step):
        return {"ka": lax.rem(line + step, lines) * PLANE + spot}

    barrier = pltpu.get_barrier_semaphore()

    @pl.loop(1, lines)
    def _(step):
        pl.semaphore_signal(barrier, inc=1, device_id=in_line(lines - step), device_id_type=MESH)

    @pl.loop(1, PLANE)
    def _(step):
        pl.semaphore_signal(barrier, inc=1, device_id=in_plane(step), device_id_type=MESH)

    loads = [
        pltpu.make_async_copy(source, held, load_sem.at[i])
        for i, (source, held) in enumerate(
            ((owner_hbm, owner), (q_hbm, q_ref), (table_hbm, table), (orb_hbm, orb), (green_hbm, green))
        )
    ]
    for load in loads:
        load.start()
    for load in loads[:3]:
        load.wait()

    owner_columns = jnp.transpose(
        jnp.broadcast_to(owner[...].astype(jnp.float32), (LANES, npts))
    )
    for tile in range(npts // LANES):
        points = lax.broadcasted_iota(jnp.int32, (npts, LANES), 1) + tile * LANES
        select[:, tile * LANES : (tile + 1) * LANES] = jnp.where(
            owner_columns == points.astype(jnp.float32), 1.0, 0.0
        ).astype(jnp.bfloat16)

    table_columns = lax.broadcasted_iota(jnp.int32, table.shape, 1)
    lane = lax.broadcasted_iota(jnp.int32, (per, LANES), 1)
    which = lax.broadcasted_iota(jnp.int32, (per, LANES), 0)
    placed = jnp.zeros((per, LANES), jnp.int32)
    for q in range(nq):
        chosen = jnp.where(table_columns == q_ref[q], table[...], 0)
        partner = jnp.sum(chosen, axis=1, keepdims=True)
        placed += jnp.where(lane == (spot * nq + q) * per + which, partner, 0)
    plane_send[0] = jnp.sum(placed, axis=0, keepdims=True)

    for load in loads[3:]:
        load.wait()
    for k in range(per):
        owned[...] = lax.dot_general(
            select[...], orb[k], (((1,), (1,)), ((), ())), preferred_element_type=jnp.float32
        ).astype(jnp.bfloat16)
        half_product = jnp.dot(
            green[k], orb[k], preferred_element_type=jnp.float32
        ).astype(jnp.bfloat16)
        projected = jnp.dot(owned[...], half_product, preferred_element_type=jnp.float32)
        projected = projected.reshape(n, rows, npts)
        send[:, k] = jnp.concatenate(
            [projected[:, :, :half], projected[:, :, half:]], axis=1
        ).astype(jnp.bfloat16)

    pl.semaphore_wait(barrier, lines - 1 + PLANE - 1)

    @pl.loop(1, lines)
    def _(step):
        pl.semaphore_signal(ready_sem, inc=1, device_id=in_line(lines - step), device_id_type=MESH)

    def block_copy(step):
        peer = lax.rem(line + step % lines, lines) * PLANE + lax.rem(spot + step // lines, PLANE)
        return pltpu.make_async_remote_copy(
            src_ref=send.at[peer],
            dst_ref=recv.at[pl.ds(me * per, per)],
            send_sem=send_sem.at[step],
            recv_sem=recv_sem.at[step],
            device_id={"ka": peer},
            device_id_type=MESH,
        )

    def plane_copy(step):
        return pltpu.make_async_remote_copy(
            src_ref=plane_send.at[0],
            dst_ref=plane_recv.at[spot],
            send_sem=plane_send_sem.at[step],
            recv_sem=plane_recv_sem.at[step],
            device_id=in_plane(step),
            device_id_type=MESH,
        )

    def line_copy(step):
        return pltpu.make_async_remote_copy(
            src_ref=line_send.at[0],
            dst_ref=line_recv.at[line],
            send_sem=line_send_sem.at[step],
            recv_sem=line_recv_sem.at[step],
            device_id=in_line(step),
            device_id_type=MESH,
        )

    @pl.loop(1, lines)
    def _(step):
        block_copy(step).start()

    @pl.loop(1, PLANE)
    def _(step):
        plane_copy(step).start()
        block_copy(step * lines).start()

    pl.semaphore_wait(ready_sem, lines - 1)

    def send_rest(first, last):
        @pl.loop(first, last)
        def _(turn):
            @pl.loop(1, lines)
            def _(step):
                block_copy(turn * lines + step).start()

    send_rest(1, PLANE // 2)

    own = pltpu.make_async_copy(send.at[me], recv.at[pl.ds(me * per, per)], local_sem.at[0])
    own.start()
    plane_own = pltpu.make_async_copy(plane_send.at[0], plane_recv.at[spot], local_sem.at[1])
    plane_own.start()
    plane_own.wait()

    @pl.loop(1, PLANE)
    def _(step):
        plane_copy(step).wait()

    line_send[0] = jnp.sum(plane_recv[...], axis=0)

    @pl.loop(1, lines)
    def _(step):
        line_copy(step).start()

    line_own = pltpu.make_async_copy(line_send.at[0], line_recv.at[line], local_sem.at[2])
    line_own.start()

    send_rest(PLANE // 2, PLANE)

    own.wait()
    line_own.wait()

    @pl.loop(1, lines)
    def _(step):
        line_copy(step).wait()

    to_scalar = pltpu.make_async_copy(line_recv, pairs, local_sem.at[3])
    to_scalar.start()
    to_scalar.wait()

    @pl.loop(1, n)
    def _(step):
        block_copy(step).wait()

    def add(device, totals):
        totals = list(totals)
        for j in range(per):
            mine = recv[device * per + j].astype(jnp.float32)
            for q in range(nq):
                at = pairs[device // PLANE, 0, (device % PLANE * nq + q) * per + j]
                totals[q] = totals[q] + mine * recv[at].astype(jnp.float32)
        return tuple(totals)

    zero = jnp.zeros(recv.shape[1:], jnp.float32)
    totals = lax.fori_loop(0, n, add, (zero,) * nq, unroll=4)
    for q in range(nq):
        scaled = totals[q] * (1.0 / (n * per))
        out_ref[:, q * npts : q * npts + half] = scaled[:rows]
        out_ref[:, q * npts + half : (q + 1) * npts] = scaled[rows:]


def solution(mesh):
    n = mesh.shape["ka"]

    def per_device(green_time, orbitals, pair_table, pair_momenta, owner_rows):
        per, norb, npts = orbitals.shape
        nq = pair_momenta.shape[0]
        rows = npts // n
        bf16, i32 = jnp.bfloat16, jnp.int32
        dma = pltpu.SemaphoreType.DMA
        out = pl.pallas_call(
            functools.partial(kernel, n),
            out_shape=jax.ShapeDtypeStruct((rows, nq * npts), jnp.float32),
            in_specs=[pl.BlockSpec(memory_space=pltpu.HBM)] * 5,
            out_specs=pl.BlockSpec(memory_space=pltpu.VMEM),
            scratch_shapes=[
                pltpu.SMEM((nq,), i32),
                pltpu.VMEM((per, norb, norb), bf16),
                pltpu.VMEM((per, norb, npts), bf16),
                pltpu.VMEM((per, n * per), i32),
                pltpu.VMEM((1, npts), i32),
                pltpu.VMEM((npts, npts), bf16),
                pltpu.VMEM((npts, norb), bf16),
                pltpu.VMEM((n, per, 2 * rows, npts // 2), bf16),
                pltpu.VMEM((n * per, 2 * rows, npts // 2), bf16),
                pltpu.VMEM((1, 1, LANES), i32),
                pltpu.VMEM((PLANE, 1, LANES), i32),
                pltpu.VMEM((1, 1, LANES), i32),
                pltpu.VMEM((n // PLANE, 1, LANES), i32),
                pltpu.SMEM((n // PLANE, 1, LANES), i32),
                dma((5,)),
                dma((n,)),
                dma((n,)),
                dma((PLANE,)),
                dma((PLANE,)),
                dma((n // PLANE,)),
                dma((n // PLANE,)),
                dma((4,)),
                pltpu.SemaphoreType.REGULAR,
            ],
            compiler_params=pltpu.CompilerParams(
                collective_id=0, has_side_effects=True, vmem_limit_bytes=56 * 1024 * 1024
            ),
            cost_estimate=pl.CostEstimate(
                flops=2 * per * npts * (norb * norb + npts * norb * 2),
                bytes_accessed=2 * per * norb * (norb + npts),
                transcendentals=0,
            ),
        )(pair_momenta, green_time, orbitals, pair_table.T, owner_rows.reshape(1, npts))
        return out.reshape(rows, nq, npts)

    return jax.shard_map(
        per_device,
        mesh=mesh,
        in_specs=(P(("ta", "ka"), None, None), P("ka", None, None), P(None, "ka"), P(), P()),
        out_specs=P(("ta", "ka"), None, None),
        check_vma=False,
    )
```

```python
import functools

import jax
import jax.numpy as jnp
from jax import lax
from jax.experimental import pallas as pl
from jax.experimental.pallas import tpu as pltpu
from jax.sharding import PartitionSpec as P

MESH = pl.DeviceIdType.MESH
PLANE = 8
LANES = 128


def kernel(
    n, q_hbm, green_hbm, orb_hbm, table_hbm, owner_hbm, out_ref,
    q_ref, green, orb, table, owner, select, owned, send, recv,
    plane_send, plane_recv, line_send, line_recv, pairs,
    load_sem, send_sem, recv_sem, plane_send_sem, plane_recv_sem, line_send_sem, line_recv_sem, local_sem, ready_sem,
):
    me = lax.axis_index("ka")
    line, spot = me // PLANE, me % PLANE
    lines = n // PLANE
    per, norb, npts = orb.shape
    nq = q_ref.shape[0]
    rows = npts // n
    half = npts // 2

    def in_plane(step):
        return {"ka": line * PLANE + lax.rem(spot + step, PLANE)}

    def in_line(step):
        return {"ka": lax.rem(line + step, lines) * PLANE + spot}

    barrier = pltpu.get_barrier_semaphore()

    @pl.loop(1, lines)
    def _(step):
        pl.semaphore_signal(barrier, inc=1, device_id=in_line(lines - step), device_id_type=MESH)

    @pl.loop(1, PLANE)
    def _(step):
        pl.semaphore_signal(barrier, inc=1, device_id=in_plane(step), device_id_type=MESH)

    loads = [
        pltpu.make_async_copy(source, held, load_sem.at[i])
        for i, (source, held) in enumerate(
            ((owner_hbm, owner), (q_hbm, q_ref), (table_hbm, table), (orb_hbm, orb), (green_hbm, green))
        )
    ]
    for load in loads:
        load.start()
    for load in loads[:3]:
        load.wait()

    owner_columns = jnp.transpose(
        jnp.broadcast_to(owner[...].astype(jnp.float32), (LANES, npts))
    )
    for tile in range(npts // LANES):
        points = lax.broadcasted_iota(jnp.int32, (npts, LANES), 1) + tile * LANES
        select[:, tile * LANES : (tile + 1) * LANES] = jnp.where(
            owner_columns == points.astype(jnp.float32), 1.0, 0.0
        ).astype(jnp.bfloat16)

    table_columns = lax.broadcasted_iota(jnp.int32, table.shape, 1)
    lane = lax.broadcasted_iota(jnp.int32, (per, LANES), 1)
    which = lax.broadcasted_iota(jnp.int32, (per, LANES), 0)
    placed = jnp.zeros((per, LANES), jnp.int32)
    for q in range(nq):
        chosen = jnp.where(table_columns == q_ref[q], table[...], 0)
        partner = jnp.sum(chosen, axis=1, keepdims=True)
        placed += jnp.where(lane == (spot * nq + q) * per + which, partner, 0)
    plane_send[0] = jnp.sum(placed, axis=0, keepdims=True)

    for load in loads[3:]:
        load.wait()
    for k in range(per):
        owned[...] = lax.dot_general(
            select[...], orb[k], (((1,), (1,)), ((), ())), preferred_element_type=jnp.float32
        ).astype(jnp.bfloat16)
        half_product = jnp.dot(
            green[k], orb[k], preferred_element_type=jnp.float32
        ).astype(jnp.bfloat16)
        projected = jnp.dot(owned[...], half_product, preferred_element_type=jnp.float32)
        projected = projected.reshape(n, rows, npts)
        send[:, k] = jnp.concatenate(
            [projected[:, :, :half], projected[:, :, half:]], axis=1
        ).astype(jnp.bfloat16)

    pl.semaphore_wait(barrier, lines - 1 + PLANE - 1)

    @pl.loop(1, lines)
    def _(step):
        pl.semaphore_signal(ready_sem, inc=1, device_id=in_line(lines - step), device_id_type=MESH)

    def block_copy(step):
        peer = lax.rem(line + step % lines, lines) * PLANE + lax.rem(spot + step // lines, PLANE)
        return pltpu.make_async_remote_copy(
            src_ref=send.at[peer],
            dst_ref=recv.at[pl.ds(me * per, per)],
            send_sem=send_sem.at[step],
            recv_sem=recv_sem.at[step],
            device_id={"ka": peer},
            device_id_type=MESH,
        )

    def plane_copy(step):
        return pltpu.make_async_remote_copy(
            src_ref=plane_send.at[0],
            dst_ref=plane_recv.at[spot],
            send_sem=plane_send_sem.at[step],
            recv_sem=plane_recv_sem.at[step],
            device_id=in_plane(step),
            device_id_type=MESH,
        )

    def line_copy(step):
        return pltpu.make_async_remote_copy(
            src_ref=line_send.at[0],
            dst_ref=line_recv.at[line],
            send_sem=line_send_sem.at[step],
            recv_sem=line_recv_sem.at[step],
            device_id=in_line(step),
            device_id_type=MESH,
        )

    @pl.loop(1, lines)
    def _(step):
        block_copy(step).start()

    @pl.loop(1, PLANE)
    def _(step):
        plane_copy(step).start()
        block_copy(step * lines).start()

    pl.semaphore_wait(ready_sem, lines - 1)

    def send_rest(first, last):
        @pl.loop(first, last)
        def _(turn):
            @pl.loop(1, lines)
            def _(step):
                block_copy(turn * lines + step).start()

    send_rest(1, PLANE // 2)

    own = pltpu.make_async_copy(send.at[me], recv.at[pl.ds(me * per, per)], local_sem.at[0])
    own.start()
    plane_own = pltpu.make_async_copy(plane_send.at[0], plane_recv.at[spot], local_sem.at[1])
    plane_own.start()
    plane_own.wait()

    @pl.loop(1, PLANE)
    def _(step):
        plane_copy(step).wait()

    line_send[0] = jnp.sum(plane_recv[...], axis=0)

    @pl.loop(1, lines)
    def _(step):
        line_copy(step).start()

    line_own = pltpu.make_async_copy(line_send.at[0], line_recv.at[line], local_sem.at[2])
    line_own.start()

    send_rest(PLANE // 2, PLANE)

    own.wait()
    line_own.wait()

    @pl.loop(1, lines)
    def _(step):
        line_copy(step).wait()

    to_scalar = pltpu.make_async_copy(line_recv, pairs, local_sem.at[3])
    to_scalar.start()
    to_scalar.wait()

    @pl.loop(1, n)
    def _(step):
        block_copy(step).wait()

    def add(row, totals):
        totals = list(totals)
        for place in range(PLANE):
            for j in range(per):
                mine = recv[(row * PLANE + place) * per + j].astype(jnp.float32)
                for q in range(nq):
                    at = pairs[row, 0, (place * nq + q) * per + j]
                    totals[q] = totals[q] + mine * recv[at].astype(jnp.float32)
        return tuple(totals)

    zero = jnp.zeros(recv.shape[1:], jnp.float32)
    totals = lax.fori_loop(0, lines, add, (zero,) * nq)
    for q in range(nq):
        scaled = totals[q] * (1.0 / (n * per))
        out_ref[:, q, :half] = scaled[:rows]
        out_ref[:, q, half:] = scaled[rows:]


def solution(mesh):
    n = mesh.shape["ka"]

    def per_device(green_time, orbitals, pair_table, pair_momenta, owner_rows):
        per, norb, npts = orbitals.shape
        nq = pair_momenta.shape[0]
        rows = npts // n
        bf16, i32 = jnp.bfloat16, jnp.int32
        dma = pltpu.SemaphoreType.DMA
        out = pl.pallas_call(
            functools.partial(kernel, n),
            out_shape=jax.ShapeDtypeStruct((rows, nq, npts), jnp.float32),
            in_specs=[pl.BlockSpec(memory_space=pltpu.HBM)] * 5,
            out_specs=pl.BlockSpec(memory_space=pltpu.VMEM),
            scratch_shapes=[
                pltpu.SMEM((nq,), i32),
                pltpu.VMEM((per, norb, norb), bf16),
                pltpu.VMEM((per, norb, npts), bf16),
                pltpu.VMEM((per, n * per), i32),
                pltpu.VMEM((1, npts), i32),
                pltpu.VMEM((npts, npts), bf16),
                pltpu.VMEM((npts, norb), bf16),
                pltpu.VMEM((n, per, 2 * rows, npts // 2), bf16),
                pltpu.VMEM((n * per, 2 * rows, npts // 2), bf16),
                pltpu.VMEM((1, 1, LANES), i32),
                pltpu.VMEM((PLANE, 1, LANES), i32),
                pltpu.VMEM((1, 1, LANES), i32),
                pltpu.VMEM((n // PLANE, 1, LANES), i32),
                pltpu.SMEM((n // PLANE, 1, LANES), i32),
                dma((5,)),
                dma((n,)),
                dma((n,)),
                dma((PLANE,)),
                dma((PLANE,)),
                dma((n // PLANE,)),
                dma((n // PLANE,)),
                dma((4,)),
                pltpu.SemaphoreType.REGULAR,
            ],
            compiler_params=pltpu.CompilerParams(
                collective_id=0, has_side_effects=True, vmem_limit_bytes=56 * 1024 * 1024
            ),
            cost_estimate=pl.CostEstimate(
                flops=2 * per * npts * (norb * norb + npts * norb * 2),
                bytes_accessed=2 * per * norb * (norb + npts),
                transcendentals=0,
            ),
        )(pair_momenta, green_time, orbitals, pair_table.T, owner_rows.reshape(1, npts))
        return out

    return jax.shard_map(
        per_device,
        mesh=mesh,
        in_specs=(P(("ta", "ka"), None, None), P("ka", None, None), P(None, "ka"), P(), P()),
        out_specs=P(("ta", "ka"), None, None),
        check_vma=False,
    )
```

```python
import functools

import jax
import jax.numpy as jnp
from jax import lax
from jax.experimental import pallas as pl
from jax.experimental.pallas import tpu as pltpu
from jax.sharding import PartitionSpec as P

MESH = pl.DeviceIdType.MESH
PLANE = 8
LANES = 128


def kernel(
    n, q_hbm, green_hbm, orb_hbm, table_hbm, owner_hbm, out_ref,
    q_ref, green, orb, table, owner, select, owned, send, recv,
    plane_send, plane_recv, line_send, line_recv, pairs,
    load_sem, send_sem, recv_sem, plane_send_sem, plane_recv_sem, line_send_sem, line_recv_sem, local_sem, ready_sem,
):
    me = lax.axis_index("ka")
    line, spot = me // PLANE, me % PLANE
    lines = n // PLANE
    per, norb, npts = orb.shape
    nq = q_ref.shape[0]
    rows = npts // n
    half = npts // 2

    def in_plane(step):
        return {"ka": line * PLANE + lax.rem(spot + step, PLANE)}

    def in_line(step):
        return {"ka": lax.rem(line + step, lines) * PLANE + spot}

    barrier = pltpu.get_barrier_semaphore()

    @pl.loop(1, lines)
    def _(step):
        pl.semaphore_signal(barrier, inc=1, device_id=in_line(lines - step), device_id_type=MESH)

    @pl.loop(1, PLANE)
    def _(step):
        pl.semaphore_signal(barrier, inc=1, device_id=in_plane(step), device_id_type=MESH)

    loads = [
        pltpu.make_async_copy(source, held, load_sem.at[i])
        for i, (source, held) in enumerate(
            ((owner_hbm, owner), (q_hbm, q_ref), (table_hbm, table), (orb_hbm, orb), (green_hbm, green))
        )
    ]
    for load in loads:
        load.start()
    for load in loads[:3]:
        load.wait()

    owner_columns = jnp.transpose(
        jnp.broadcast_to(owner[...].astype(jnp.float32), (LANES, npts))
    )
    for tile in range(npts // LANES):
        points = lax.broadcasted_iota(jnp.int32, (npts, LANES), 1) + tile * LANES
        select[:, tile * LANES : (tile + 1) * LANES] = jnp.where(
            owner_columns == points.astype(jnp.float32), 1.0, 0.0
        ).astype(jnp.bfloat16)

    table_columns = lax.broadcasted_iota(jnp.int32, table.shape, 1)
    lane = lax.broadcasted_iota(jnp.int32, (per, LANES), 1)
    which = lax.broadcasted_iota(jnp.int32, (per, LANES), 0)
    placed = jnp.zeros((per, LANES), jnp.int32)
    for q in range(nq):
        chosen = jnp.where(table_columns == q_ref[q], table[...], 0)
        partner = jnp.sum(chosen, axis=1, keepdims=True)
        placed += jnp.where(lane == (spot * nq + q) * per + which, partner, 0)
    plane_send[0] = jnp.sum(placed, axis=0, keepdims=True)

    for load in loads[3:]:
        load.wait()
    for k in range(per):
        owned[...] = lax.dot_general(
            select[...], orb[k], (((1,), (1,)), ((), ())), preferred_element_type=jnp.float32
        ).astype(jnp.bfloat16)
        half_product = jnp.dot(
            green[k], orb[k], preferred_element_type=jnp.float32
        ).astype(jnp.bfloat16)
        projected = jnp.dot(owned[...], half_product, preferred_element_type=jnp.float32)
        projected = projected.reshape(n, rows, npts)
        send[:, k] = jnp.concatenate(
            [projected[:, :, :half], projected[:, :, half:]], axis=1
        ).astype(jnp.bfloat16)

    pl.semaphore_wait(barrier, lines - 1 + PLANE - 1)

    @pl.loop(1, lines)
    def _(step):
        pl.semaphore_signal(ready_sem, inc=1, device_id=in_line(lines - step), device_id_type=MESH)

    def block_copy(step):
        peer = lax.rem(line + step % lines, lines) * PLANE + lax.rem(spot + step // lines, PLANE)
        return pltpu.make_async_remote_copy(
            src_ref=send.at[peer],
            dst_ref=recv.at[pl.ds(me * per, per)],
            send_sem=send_sem.at[step],
            recv_sem=recv_sem.at[step],
            device_id={"ka": peer},
            device_id_type=MESH,
        )

    def plane_copy(step):
        return pltpu.make_async_remote_copy(
            src_ref=plane_send.at[0],
            dst_ref=plane_recv.at[spot],
            send_sem=plane_send_sem.at[step],
            recv_sem=plane_recv_sem.at[step],
            device_id=in_plane(step),
            device_id_type=MESH,
        )

    def line_copy(step):
        return pltpu.make_async_remote_copy(
            src_ref=line_send.at[0],
            dst_ref=line_recv.at[line],
            send_sem=line_send_sem.at[step],
            recv_sem=line_recv_sem.at[step],
            device_id=in_line(step),
            device_id_type=MESH,
        )

    @pl.loop(1, lines)
    def _(step):
        block_copy(step).start()

    @pl.loop(1, PLANE)
    def _(step):
        plane_copy(step).start()
        block_copy(step * lines).start()

    pl.semaphore_wait(ready_sem, lines - 1)

    def send_rest(first, last):
        @pl.loop(first, last)
        def _(turn):
            @pl.loop(1, lines)
            def _(step):
                block_copy(turn * lines + step).start()

    send_rest(1, PLANE // 2)

    own = pltpu.make_async_copy(send.at[me], recv.at[pl.ds(me * per, per)], local_sem.at[0])
    own.start()
    plane_own = pltpu.make_async_copy(plane_send.at[0], plane_recv.at[spot], local_sem.at[1])
    plane_own.start()
    plane_own.wait()

    @pl.loop(1, PLANE)
    def _(step):
        plane_copy(step).wait()

    line_send[0] = jnp.sum(plane_recv[...], axis=0)

    @pl.loop(1, lines)
    def _(step):
        line_copy(step).start()

    line_own = pltpu.make_async_copy(line_send.at[0], line_recv.at[line], local_sem.at[2])
    line_own.start()

    send_rest(PLANE // 2, PLANE)

    own.wait()
    line_own.wait()

    @pl.loop(1, lines)
    def _(step):
        line_copy(step).wait()

    to_scalar = pltpu.make_async_copy(line_recv, pairs, local_sem.at[3])
    to_scalar.start()
    to_scalar.wait()

    @pl.loop(1, n)
    def _(step):
        block_copy(step).wait()

    def add(row, totals):
        totals = list(totals)
        for place in range(PLANE):
            for j in range(per):
                mine = recv[(row * PLANE + place) * per + j].astype(jnp.float32)
                for q in range(nq):
                    at = pairs[row, 0, (place * nq + q) * per + j]
                    totals[q] = totals[q] + mine * recv[at].astype(jnp.float32)
        return tuple(totals)

    zero = jnp.zeros(recv.shape[1:], jnp.float32)
    totals = lax.fori_loop(0, lines, add, (zero,) * nq)
    for q in range(nq):
        scaled = totals[q] * (1.0 / (n * per))
        out_ref[:, q, :half] = scaled[:rows]
        out_ref[:, q, half:] = scaled[rows:]


def solution(mesh):
    n = mesh.shape["ka"]

    def per_device(green_time, orbitals, pair_table, pair_momenta, owner_rows):
        per, norb, npts = orbitals.shape
        nq = pair_momenta.shape[0]
        rows = npts // n
        bf16, i32 = jnp.bfloat16, jnp.int32
        dma = pltpu.SemaphoreType.DMA
        out = pl.pallas_call(
            functools.partial(kernel, n),
            out_shape=jax.ShapeDtypeStruct((rows, nq, npts), jnp.float32),
            in_specs=[pl.BlockSpec(memory_space=pltpu.HBM)] * 5,
            out_specs=pl.BlockSpec(memory_space=pltpu.VMEM),
            scratch_shapes=[
                pltpu.SMEM((nq,), i32),
                pltpu.VMEM((per, norb, norb), bf16),
                pltpu.VMEM((per, norb, npts), bf16),
                pltpu.VMEM((per, n * per), i32),
                pltpu.VMEM((1, npts), i32),
                pltpu.VMEM((npts, npts), bf16),
                pltpu.VMEM((npts, norb), bf16),
                pltpu.VMEM((n, per, 2 * rows, npts // 2), bf16),
                pltpu.VMEM((n * per, 2 * rows, npts // 2), bf16),
                pltpu.VMEM((1, 1, LANES), i32),
                pltpu.VMEM((PLANE, 1, LANES), i32),
                pltpu.VMEM((1, 1, LANES), i32),
                pltpu.VMEM((n // PLANE, 1, LANES), i32),
                pltpu.SMEM((n // PLANE, 1, LANES), i32),
                dma((5,)),
                dma((n,)),
                dma((n,)),
                dma((PLANE,)),
                dma((PLANE,)),
                dma((n // PLANE,)),
                dma((n // PLANE,)),
                dma((4,)),
                pltpu.SemaphoreType.REGULAR,
            ],
            compiler_params=pltpu.CompilerParams(
                collective_id=0, has_side_effects=True, vmem_limit_bytes=32 * 1024 * 1024
            ),
            cost_estimate=pl.CostEstimate(
                flops=2 * per * npts * (norb * norb + npts * norb * 2),
                bytes_accessed=2 * per * norb * (norb + npts),
                transcendentals=0,
            ),
        )(
            *(
                pltpu.with_memory_space_constraint(operand, pltpu.HBM)
                for operand in (pair_momenta, green_time, orbitals, pair_table.T, owner_rows.reshape(1, npts))
            )
        )
        return out

    return jax.shard_map(
        per_device,
        mesh=mesh,
        in_specs=(P(("ta", "ka"), None, None), P("ka", None, None), P(None, "ka"), P(), P()),
        out_specs=P(("ta", "ka"), None, None),
        check_vma=False,
    )
```

```python
import functools

import jax
import jax.numpy as jnp
from jax import lax
from jax.experimental import pallas as pl
from jax.experimental.pallas import tpu as pltpu
from jax.sharding import PartitionSpec as P

MESH = pl.DeviceIdType.MESH
PLANE = 8
LANES = 128
EARLY = 6


def kernel(
    n, q_hbm, green_hbm, orb_hbm, table_hbm, owner_hbm, out_ref,
    q_ref, green, orb, table, owner, select, owned, send, early, full,
    plane_send, plane_recv, line_send, line_recv, places, pairs,
    load_sem, send_sem, recv_sem, plane_send_sem, plane_recv_sem, line_send_sem, line_recv_sem, local_sem, ready_sem,
):
    me = lax.axis_index("ka")
    line, spot = me // PLANE, me % PLANE
    lines = n // PLANE
    per, norb, npts = orb.shape
    nq = q_ref.shape[0]
    rows = npts // n
    half = npts // 2

    def in_plane(step):
        return {"ka": line * PLANE + lax.rem(spot + step, PLANE)}

    def in_line(step):
        return {"ka": lax.rem(line + step, lines) * PLANE + spot}

    small = [
        pltpu.make_async_copy(source, held, load_sem.at[i])
        for i, (source, held) in enumerate(((owner_hbm, owner), (q_hbm, q_ref), (table_hbm, table)))
    ]
    loads = [
        (
            pltpu.make_async_copy(orb_hbm.at[k], orb.at[k], load_sem.at[3 + k]),
            pltpu.make_async_copy(green_hbm.at[k], green.at[k], load_sem.at[3 + per + k]),
        )
        for k in range(per)
    ]
    for load in small + [load for both in loads for load in both]:
        load.start()

    barrier = pltpu.get_barrier_semaphore()

    @pl.loop(1, lines)
    def _(step):
        pl.semaphore_signal(barrier, inc=1, device_id=in_line(lines - step), device_id_type=MESH)

    @pl.loop(1, PLANE)
    def _(step):
        pl.semaphore_signal(barrier, inc=1, device_id=in_plane(step), device_id_type=MESH)

    for load in small:
        load.wait()

    owner_columns = jnp.transpose(
        jnp.broadcast_to(owner[...].astype(jnp.float32), (LANES, npts))
    )
    for tile in range(npts // LANES):
        points = lax.broadcasted_iota(jnp.int32, (npts, LANES), 1) + tile * LANES
        select[:, tile * LANES : (tile + 1) * LANES] = jnp.where(
            owner_columns == points.astype(jnp.float32), 1.0, 0.0
        ).astype(jnp.bfloat16)

    table_columns = lax.broadcasted_iota(jnp.int32, table.shape, 1)
    lane = lax.broadcasted_iota(jnp.int32, (per, LANES), 1)
    which = lax.broadcasted_iota(jnp.int32, (per, LANES), 0)
    placed = jnp.zeros((per, LANES), jnp.int32)
    for q in range(nq):
        chosen = jnp.where(table_columns == q_ref[q], table[...], 0)
        partner = jnp.sum(chosen, axis=1, keepdims=True)
        placed += jnp.where(lane == (spot * nq + q) * per + which, partner, 0)
    plane_send[0] = jnp.sum(placed, axis=0, keepdims=True)

    for k in range(per):
        for load in loads[k]:
            load.wait()
        owned[...] = lax.dot_general(
            select[...], orb[k], (((1,), (1,)), ((), ())), preferred_element_type=jnp.float32
        ).astype(jnp.bfloat16)
        half_product = jnp.dot(
            green[k], orb[k], preferred_element_type=jnp.float32
        ).astype(jnp.bfloat16)
        projected = jnp.dot(owned[...], half_product, preferred_element_type=jnp.float32)
        projected = projected.reshape(n, rows, npts)
        send[:, k] = jnp.concatenate(
            [projected[:, :, :half], projected[:, :, half:]], axis=1
        ).astype(jnp.bfloat16)

    pl.semaphore_wait(barrier, lines - 1 + PLANE - 1)

    @pl.loop(1, lines)
    def _(step):
        pl.semaphore_signal(ready_sem, inc=1, device_id=in_line(lines - step), device_id_type=MESH)

    def arrival(turn, row):
        place = (turn * lines + row) * per
        return (early if turn < EARLY else full).at[pl.ds(place, per)]

    def block_copy(turn, step):
        peer = lax.rem(line + step, lines) * PLANE + lax.rem(spot + turn, PLANE)
        return pltpu.make_async_remote_copy(
            src_ref=send.at[peer],
            dst_ref=arrival(turn, line),
            send_sem=send_sem.at[turn * lines + step],
            recv_sem=recv_sem.at[turn * lines + step],
            device_id={"ka": peer},
            device_id_type=MESH,
        )

    def plane_copy(step):
        return pltpu.make_async_remote_copy(
            src_ref=plane_send.at[0],
            dst_ref=plane_recv.at[spot],
            send_sem=plane_send_sem.at[step],
            recv_sem=plane_recv_sem.at[step],
            device_id=in_plane(step),
            device_id_type=MESH,
        )

    def line_copy(step):
        return pltpu.make_async_remote_copy(
            src_ref=line_send.at[0],
            dst_ref=line_recv.at[line],
            send_sem=line_send_sem.at[step],
            recv_sem=line_recv_sem.at[step],
            device_id=in_line(step),
            device_id_type=MESH,
        )

    @pl.loop(1, lines)
    def _(step):
        block_copy(0, step).start()

    for turn in range(1, PLANE):
        plane_copy(turn).start()
        block_copy(turn, 0).start()

    pl.semaphore_wait(ready_sem, lines - 1)

    def send_rest(turns):
        for turn in turns:
            @pl.loop(1, lines)
            def _(step):
                block_copy(turn, lines - step if turn % 2 else step).start()

    send_rest(range(1, PLANE // 2))

    own = pltpu.make_async_copy(send.at[me], arrival(0, line), local_sem.at[0])
    own.start()
    plane_own = pltpu.make_async_copy(plane_send.at[0], plane_recv.at[spot], local_sem.at[1])
    plane_own.start()
    plane_own.wait()

    @pl.loop(1, PLANE)
    def _(step):
        plane_copy(step).wait()

    line_send[0] = jnp.sum(plane_recv[...], axis=0)

    @pl.loop(1, lines)
    def _(step):
        line_copy(step).start()

    line_own = pltpu.make_async_copy(line_send.at[0], line_recv.at[line], local_sem.at[2])
    line_own.start()

    send_rest(range(PLANE // 2, PLANE))

    own.wait()
    line_own.wait()

    @pl.loop(1, lines)
    def _(step):
        line_copy(step).wait()

    partner = line_recv[...]
    turn_of = (spot + PLANE - (partner // per) % PLANE) % PLANE
    place = (turn_of * lines + partner // (per * PLANE)) * per + partner % per
    places[0] = jnp.where(turn_of < EARLY, place, EARLY * lines * per)
    places[1] = place
    to_scalar = pltpu.make_async_copy(places, pairs, local_sem.at[3])
    to_scalar.start()
    to_scalar.wait()

    zero = jnp.zeros(early.shape[1:], jnp.float32)
    early[EARLY * lines * per] = zero.astype(early.dtype)

    def wait_for(turns):
        for turn in turns:
            @pl.loop(0 if turn else 1, lines)
            def _(step):
                block_copy(turn, step).wait()

    def pair_sum(totals, turns, held, table):
        def add(row, totals):
            totals = list(totals)
            for turn in turns:
                lanes = lax.rem(spot + PLANE - turn, PLANE) * nq * per
                for j in range(per):
                    at = (turn * lines + row) * per + j
                    mine = held[at].astype(jnp.float32)
                    if held is early:
                        full[at] = (mine + mine).astype(full.dtype)
                    for q in range(nq):
                        other = held[pairs[table, row, 0, lanes + q * per + j]]
                        totals[q] = totals[q] + mine * other.astype(jnp.float32)
            return tuple(totals)

        return lax.fori_loop(0, lines, add, totals)

    wait_for(range(EARLY))
    totals = pair_sum((zero,) * nq, range(EARLY), early, 0)
    wait_for(range(EARLY, PLANE))
    totals = pair_sum(totals, range(EARLY, PLANE), full, 1)
    for q in range(nq):
        scaled = totals[q] * (1.0 / (n * per))
        out_ref[:, q, :half] = scaled[:rows]
        out_ref[:, q, half:] = scaled[rows:]


def solution(mesh):
    n = mesh.shape["ka"]

    def per_device(green_time, orbitals, pair_table, pair_momenta, owner_rows):
        per, norb, npts = orbitals.shape
        nq = pair_momenta.shape[0]
        rows = npts // n
        bf16, i32 = jnp.bfloat16, jnp.int32
        dma = pltpu.SemaphoreType.DMA
        out = pl.pallas_call(
            functools.partial(kernel, n),
            out_shape=jax.ShapeDtypeStruct((rows, nq, npts), jnp.float32),
            in_specs=[pl.BlockSpec(memory_space=pltpu.HBM)] * 5,
            out_specs=pl.BlockSpec(memory_space=pltpu.VMEM),
            scratch_shapes=[
                pltpu.SMEM((nq,), i32),
                pltpu.VMEM((per, norb, norb), bf16),
                pltpu.VMEM((per, norb, npts), bf16),
                pltpu.VMEM((per, n * per), i32),
                pltpu.VMEM((1, npts), i32),
                pltpu.VMEM((npts, npts), bf16),
                pltpu.VMEM((npts, norb), bf16),
                pltpu.VMEM((n, per, 2 * rows, npts // 2), bf16),
                pltpu.VMEM(((EARLY * n // PLANE + 1) * per, 2 * rows, npts // 2), bf16),
                pltpu.VMEM((n * per, 2 * rows, npts // 2), bf16),
                pltpu.VMEM((1, 1, LANES), i32),
                pltpu.VMEM((PLANE, 1, LANES), i32),
                pltpu.VMEM((1, 1, LANES), i32),
                pltpu.VMEM((n // PLANE, 1, LANES), i32),
                pltpu.VMEM((2, n // PLANE, 1, LANES), i32),
                pltpu.SMEM((2, n // PLANE, 1, LANES), i32),
                dma((3 + 2 * per,)),
                dma((n,)),
                dma((n,)),
                dma((PLANE,)),
                dma((PLANE,)),
                dma((n // PLANE,)),
                dma((n // PLANE,)),
                dma((4,)),
                pltpu.SemaphoreType.REGULAR,
            ],
            compiler_params=pltpu.CompilerParams(
                collective_id=0, has_side_effects=True, vmem_limit_bytes=32 * 1024 * 1024
            ),
            cost_estimate=pl.CostEstimate(
                flops=2 * per * npts * (norb * norb + npts * norb * 2),
                bytes_accessed=2 * per * norb * (norb + npts),
                transcendentals=0,
            ),
        )(
            *(
                pltpu.with_memory_space_constraint(operand, pltpu.HBM)
                for operand in (pair_momenta, green_time, orbitals, pair_table.T, owner_rows.reshape(1, npts))
            )
        )
        return out

    return jax.shard_map(
        per_device,
        mesh=mesh,
        in_specs=(P(("ta", "ka"), None, None), P("ka", None, None), P(None, "ka"), P(), P()),
        out_specs=P(("ta", "ka"), None, None),
        check_vma=False,
    )
```

```python
import functools

import jax
import jax.numpy as jnp
from jax import lax
from jax.experimental import pallas as pl
from jax.experimental.pallas import tpu as pltpu
from jax.sharding import PartitionSpec as P

MESH = pl.DeviceIdType.MESH
PLANE = 8
LANES = 128
EARLY = 6


def kernel(
    n, q_hbm, green_hbm, orb_hbm, table_hbm, owner_hbm, out_ref,
    q_ref, green, orb, table, owner, owner_columns, select, half_product, send, early, full,
    plane_send, plane_recv, line_send, line_recv, places, pairs,
    load_sem, send_sem, recv_sem, plane_send_sem, plane_recv_sem, line_send_sem, line_recv_sem, local_sem, ready_sem,
):
    me = lax.axis_index("ka")
    line, spot = me // PLANE, me % PLANE
    lines = n // PLANE
    per, norb, npts = orb.shape
    nq = q_ref.shape[0]
    rows = npts // n
    half = npts // 2

    def in_plane(step):
        return {"ka": line * PLANE + lax.rem(spot + step, PLANE)}

    def in_line(step):
        return {"ka": lax.rem(line + step, lines) * PLANE + spot}

    small = [
        pltpu.make_async_copy(source, held, load_sem.at[i])
        for i, (source, held) in enumerate(((owner_hbm, owner), (q_hbm, q_ref), (table_hbm, table)))
    ]
    loads = [
        (
            pltpu.make_async_copy(orb_hbm.at[k], orb.at[k], load_sem.at[3 + k]),
            pltpu.make_async_copy(green_hbm.at[k], green.at[k], load_sem.at[3 + per + k]),
        )
        for k in range(per)
    ]
    for load in small + [load for both in loads for load in both]:
        load.start()

    barrier = pltpu.get_barrier_semaphore()

    @pl.loop(1, lines)
    def _(step):
        pl.semaphore_signal(barrier, inc=1, device_id=in_line(lines - step), device_id_type=MESH)

    @pl.loop(1, PLANE)
    def _(step):
        pl.semaphore_signal(barrier, inc=1, device_id=in_plane(step), device_id_type=MESH)

    for load in small:
        load.wait()

    owner_columns[...] = jnp.transpose(
        jnp.broadcast_to(owner[...].astype(jnp.float32), (LANES, npts))
    ).reshape(n, rows, LANES)

    def project(first, last):
        for turn in range(first, last):
            place = lax.rem(spot + turn, PLANE)
            owners = jnp.concatenate([owner_columns[row * PLANE + place] for row in range(lines)], axis=0)
            for tile in range(npts // LANES):
                points = lax.broadcasted_iota(jnp.int32, owners.shape, 1) + tile * LANES
                select[turn * lines * rows : (turn + 1) * lines * rows, tile * LANES : (tile + 1) * LANES] = (
                    jnp.where(owners == points.astype(jnp.float32), 1.0, 0.0).astype(jnp.bfloat16)
                )
        for k in range(per):
            if first == 0:
                for load in loads[k]:
                    load.wait()
                half_product[k] = jnp.dot(
                    green[k], orb[k], preferred_element_type=jnp.float32
                ).astype(jnp.bfloat16)
            owned = lax.dot_general(
                select[first * lines * rows : last * lines * rows, :],
                orb[k],
                (((1,), (1,)), ((), ())),
                preferred_element_type=jnp.float32,
            ).astype(jnp.bfloat16)
            projected = jnp.dot(owned, half_product[k], preferred_element_type=jnp.float32)
            projected = projected.reshape((last - first) * lines, rows, npts)
            send[first * lines : last * lines, k] = jnp.concatenate(
                [projected[:, :, :half], projected[:, :, half:]], axis=1
            ).astype(jnp.bfloat16)

    project(0, 1)

    pl.semaphore_wait(barrier, lines - 1 + PLANE - 1)


    def arrival(turn, row):
        place = (turn * lines + row) * per
        return (early if turn < EARLY else full).at[pl.ds(place, per)]

    def block_copy(turn, step):
        peer = lax.rem(line + step, lines) * PLANE + lax.rem(spot + turn, PLANE)
        return pltpu.make_async_remote_copy(
            src_ref=send.at[turn * lines + lax.rem(line + step, lines)],
            dst_ref=arrival(turn, line),
            send_sem=send_sem.at[turn * lines + step],
            recv_sem=recv_sem.at[turn * lines + step],
            device_id={"ka": peer},
            device_id_type=MESH,
        )

    def plane_copy(step):
        return pltpu.make_async_remote_copy(
            src_ref=plane_send.at[0],
            dst_ref=plane_recv.at[spot],
            send_sem=plane_send_sem.at[step],
            recv_sem=plane_recv_sem.at[step],
            device_id=in_plane(step),
            device_id_type=MESH,
        )

    def line_copy(step):
        return pltpu.make_async_remote_copy(
            src_ref=line_send.at[0],
            dst_ref=line_recv.at[line],
            send_sem=line_send_sem.at[step],
            recv_sem=line_recv_sem.at[step],
            device_id=in_line(step),
            device_id_type=MESH,
        )

    @pl.loop(1, lines)
    def _(step):
        block_copy(0, step).start()

    @pl.loop(1, lines)
    def _(step):
        pl.semaphore_signal(ready_sem, inc=1, device_id=in_line(lines - step), device_id_type=MESH)

    table_columns = lax.broadcasted_iota(jnp.int32, table.shape, 1)
    lane = lax.broadcasted_iota(jnp.int32, (per, LANES), 1)
    which = lax.broadcasted_iota(jnp.int32, (per, LANES), 0)
    placed = jnp.zeros((per, LANES), jnp.int32)
    for q in range(nq):
        chosen = jnp.where(table_columns == q_ref[q], table[...], 0)
        partner = jnp.sum(chosen, axis=1, keepdims=True)
        placed += jnp.where(lane == (spot * nq + q) * per + which, partner, 0)
    plane_send[0] = jnp.sum(placed, axis=0, keepdims=True)

    for turn in range(1, PLANE):
        plane_copy(turn).start()

    project(1, PLANE)
    for turn in range(1, PLANE):
        block_copy(turn, 0).start()
    pl.semaphore_wait(ready_sem, lines - 1)

    def send_rest(turns):
        for turn in turns:
            @pl.loop(1, lines)
            def _(step):
                block_copy(turn, lines - step if turn % 2 else step).start()

    send_rest(range(1, PLANE // 2))

    own = pltpu.make_async_copy(send.at[line], arrival(0, line), local_sem.at[0])
    own.start()
    plane_own = pltpu.make_async_copy(plane_send.at[0], plane_recv.at[spot], local_sem.at[1])
    plane_own.start()
    plane_own.wait()

    @pl.loop(1, PLANE)
    def _(step):
        plane_copy(step).wait()

    line_send[0] = jnp.sum(plane_recv[...], axis=0)

    @pl.loop(1, lines)
    def _(step):
        line_copy(step).start()

    line_own = pltpu.make_async_copy(line_send.at[0], line_recv.at[line], local_sem.at[2])
    line_own.start()

    send_rest(range(PLANE // 2, PLANE))

    own.wait()
    line_own.wait()

    @pl.loop(1, lines)
    def _(step):
        line_copy(step).wait()

    partner = line_recv[...]
    turn_of = (spot + PLANE - (partner // per) % PLANE) % PLANE
    place = (turn_of * lines + partner // (per * PLANE)) * per + partner % per
    places[0] = jnp.where(turn_of < EARLY, place, EARLY * lines * per)
    places[1] = place
    to_scalar = pltpu.make_async_copy(places, pairs, local_sem.at[3])
    to_scalar.start()
    to_scalar.wait()

    zero = jnp.zeros(early.shape[1:], jnp.float32)
    early[EARLY * lines * per] = zero.astype(early.dtype)

    def wait_for(turns):
        for turn in turns:
            @pl.loop(0 if turn else 1, lines)
            def _(step):
                block_copy(turn, step).wait()

    def pair_sum(totals, turns, held, table):
        def add(row, totals):
            totals = list(totals)
            for turn in turns:
                lanes = lax.rem(spot + PLANE - turn, PLANE) * nq * per
                for j in range(per):
                    at = (turn * lines + row) * per + j
                    mine = held[at].astype(jnp.float32)
                    if held is early:
                        full[at] = (mine + mine).astype(full.dtype)
                    for q in range(nq):
                        other = held[pairs[table, row, 0, lanes + q * per + j]]
                        totals[q] = totals[q] + mine * other.astype(jnp.float32)
            return tuple(totals)

        return lax.fori_loop(0, lines, add, totals)

    wait_for(range(EARLY))
    totals = pair_sum((zero,) * nq, range(EARLY), early, 0)
    wait_for(range(EARLY, PLANE))
    totals = pair_sum(totals, range(EARLY, PLANE), full, 1)
    for q in range(nq):
        scaled = totals[q] * (1.0 / (n * per))
        out_ref[:, q, :half] = scaled[:rows]
        out_ref[:, q, half:] = scaled[rows:]


def solution(mesh):
    n = mesh.shape["ka"]

    def per_device(green_time, orbitals, pair_table, pair_momenta, owner_rows):
        per, norb, npts = orbitals.shape
        nq = pair_momenta.shape[0]
        rows = npts // n
        bf16, i32 = jnp.bfloat16, jnp.int32
        dma = pltpu.SemaphoreType.DMA
        out = pl.pallas_call(
            functools.partial(kernel, n),
            out_shape=jax.ShapeDtypeStruct((rows, nq, npts), jnp.float32),
            in_specs=[pl.BlockSpec(memory_space=pltpu.HBM)] * 5,
            out_specs=pl.BlockSpec(memory_space=pltpu.VMEM),
            scratch_shapes=[
                pltpu.SMEM((nq,), i32),
                pltpu.VMEM((per, norb, norb), bf16),
                pltpu.VMEM((per, norb, npts), bf16),
                pltpu.VMEM((per, n * per), i32),
                pltpu.VMEM((1, npts), i32),
                pltpu.VMEM((n, rows, LANES), jnp.float32),
                pltpu.VMEM((npts, npts), bf16),
                pltpu.VMEM((per, norb, npts), bf16),
                pltpu.VMEM((n, per, 2 * rows, npts // 2), bf16),
                pltpu.VMEM(((EARLY * n // PLANE + 1) * per, 2 * rows, npts // 2), bf16),
                pltpu.VMEM((n * per, 2 * rows, npts // 2), bf16),
                pltpu.VMEM((1, 1, LANES), i32),
                pltpu.VMEM((PLANE, 1, LANES), i32),
                pltpu.VMEM((1, 1, LANES), i32),
                pltpu.VMEM((n // PLANE, 1, LANES), i32),
                pltpu.VMEM((2, n // PLANE, 1, LANES), i32),
                pltpu.SMEM((2, n // PLANE, 1, LANES), i32),
                dma((3 + 2 * per,)),
                dma((n,)),
                dma((n,)),
                dma((PLANE,)),
                dma((PLANE,)),
                dma((n // PLANE,)),
                dma((n // PLANE,)),
                dma((4,)),
                pltpu.SemaphoreType.REGULAR,
            ],
            compiler_params=pltpu.CompilerParams(
                collective_id=0, has_side_effects=True, vmem_limit_bytes=32 * 1024 * 1024
            ),
            cost_estimate=pl.CostEstimate(
                flops=2 * per * npts * (norb * norb + npts * norb * 2),
                bytes_accessed=2 * per * norb * (norb + npts),
                transcendentals=0,
            ),
        )(
            *(
                pltpu.with_memory_space_constraint(operand, pltpu.HBM)
                for operand in (pair_momenta, green_time, orbitals, pair_table.T, owner_rows.reshape(1, npts))
            )
        )
        return out

    return jax.shard_map(
        per_device,
        mesh=mesh,
        in_specs=(P(("ta", "ka"), None, None), P("ka", None, None), P(None, "ka"), P(), P()),
        out_specs=P(("ta", "ka"), None, None),
        check_vma=False,
    )
```

```python
import functools

import jax
import jax.numpy as jnp
from jax import lax
from jax.experimental import pallas as pl
from jax.experimental.pallas import tpu as pltpu
from jax.sharding import PartitionSpec as P

MESH = pl.DeviceIdType.MESH
PLANE = 8
LANES = 128
EARLY = 6


def kernel(
    n, q_hbm, green_hbm, orb_hbm, table_hbm, owner_hbm, out_ref,
    q_ref, green, orb, table, owner, owner_columns, select, half_product, send, early, full,
    plane_send, plane_recv, line_send, line_recv, places, pairs,
    load_sem, send_sem, recv_sem, plane_send_sem, plane_recv_sem, line_send_sem, line_recv_sem, local_sem, ready_sem,
):
    me = lax.axis_index("ka")
    line, spot = me // PLANE, me % PLANE
    lines = n // PLANE
    per, norb, npts = orb.shape
    nq = q_ref.shape[0]
    rows = npts // n
    half = npts // 2

    def in_plane(step):
        return {"ka": line * PLANE + lax.rem(spot + step, PLANE)}

    def in_line(step):
        return {"ka": lax.rem(line + step, lines) * PLANE + spot}

    small = [
        pltpu.make_async_copy(source, held, load_sem.at[i])
        for i, (source, held) in enumerate(((owner_hbm, owner), (q_hbm, q_ref), (table_hbm, table)))
    ]
    loads = [
        (
            pltpu.make_async_copy(orb_hbm.at[k], orb.at[k], load_sem.at[3 + k]),
            pltpu.make_async_copy(green_hbm.at[k], green.at[k], load_sem.at[3 + per + k]),
        )
        for k in range(per)
    ]
    for load in small + [load for both in loads for load in both]:
        load.start()

    barrier = pltpu.get_barrier_semaphore()

    @pl.loop(1, lines)
    def _(step):
        pl.semaphore_signal(barrier, inc=1, device_id=in_line(lines - step), device_id_type=MESH)

    @pl.loop(1, PLANE)
    def _(step):
        pl.semaphore_signal(barrier, inc=1, device_id=in_plane(step), device_id_type=MESH)

    for load in small:
        load.wait()

    owner_columns[...] = jnp.transpose(
        jnp.broadcast_to(owner[...].astype(jnp.float32), (LANES, npts))
    ).reshape(n, rows, LANES)

    def project(first, last):
        for turn in range(first, last):
            place = lax.rem(spot + turn, PLANE)
            owners = jnp.concatenate([owner_columns[row * PLANE + place] for row in range(lines)], axis=0)
            for tile in range(npts // LANES):
                points = lax.broadcasted_iota(jnp.int32, owners.shape, 1) + tile * LANES
                select[turn * lines * rows : (turn + 1) * lines * rows, tile * LANES : (tile + 1) * LANES] = (
                    jnp.where(owners == points.astype(jnp.float32), 1.0, 0.0).astype(jnp.bfloat16)
                )
        for k in range(per):
            if first == 0:
                for load in loads[k]:
                    load.wait()
                half_product[k] = jnp.dot(
                    green[k], orb[k], preferred_element_type=jnp.float32
                ).astype(jnp.bfloat16)
            owned = lax.dot_general(
                select[first * lines * rows : last * lines * rows, :],
                orb[k],
                (((1,), (1,)), ((), ())),
                preferred_element_type=jnp.float32,
            ).astype(jnp.bfloat16)
            projected = jnp.dot(owned, half_product[k], preferred_element_type=jnp.float32)
            projected = projected.reshape((last - first) * lines, rows, npts)
            send[first * lines : last * lines, k] = jnp.concatenate(
                [projected[:, :, :half], projected[:, :, half:]], axis=1
            ).astype(jnp.bfloat16)

    project(0, 1)

    pl.semaphore_wait(barrier, lines - 1 + PLANE - 1)


    def arrival(turn, row):
        place = (turn * lines + row) * per
        return (early if turn < EARLY else full).at[pl.ds(place, per)]

    def block_copy(turn, step):
        peer = lax.rem(line + step, lines) * PLANE + lax.rem(spot + turn, PLANE)
        return pltpu.make_async_remote_copy(
            src_ref=send.at[turn * lines + lax.rem(line + step, lines)],
            dst_ref=arrival(turn, line),
            send_sem=send_sem.at[turn * lines + step],
            recv_sem=recv_sem.at[turn * lines + step],
            device_id={"ka": peer},
            device_id_type=MESH,
        )

    def plane_copy(step):
        return pltpu.make_async_remote_copy(
            src_ref=plane_send.at[0],
            dst_ref=plane_recv.at[spot],
            send_sem=plane_send_sem.at[step],
            recv_sem=plane_recv_sem.at[step],
            device_id=in_plane(step),
            device_id_type=MESH,
        )

    def line_copy(step):
        return pltpu.make_async_remote_copy(
            src_ref=line_send.at[0],
            dst_ref=line_recv.at[line],
            send_sem=line_send_sem.at[step],
            recv_sem=line_recv_sem.at[step],
            device_id=in_line(step),
            device_id_type=MESH,
        )

    @pl.loop(1, lines)
    def _(step):
        block_copy(0, step).start()

    @pl.loop(1, lines)
    def _(step):
        pl.semaphore_signal(ready_sem, inc=1, device_id=in_line(lines - step), device_id_type=MESH)

    table_columns = lax.broadcasted_iota(jnp.int32, table.shape, 1)
    lane = lax.broadcasted_iota(jnp.int32, (per, LANES), 1)
    which = lax.broadcasted_iota(jnp.int32, (per, LANES), 0)
    placed = jnp.zeros((per, LANES), jnp.int32)
    for q in range(nq):
        chosen = jnp.where(table_columns == q_ref[q], table[...], 0)
        partner = jnp.sum(chosen, axis=1, keepdims=True)
        placed += jnp.where(lane == (spot * nq + q) * per + which, partner, 0)
    plane_send[0] = jnp.sum(placed, axis=0, keepdims=True)

    for turn in range(1, PLANE):
        plane_copy(turn).start()

    project(1, PLANE)
    for turn in range(1, PLANE):
        block_copy(turn, 0).start()
    pl.semaphore_wait(ready_sem, lines - 1)

    def send_rest(turns):
        for turn in turns:
            @pl.loop(1, lines)
            def _(step):
                block_copy(turn, lines - step if turn % 2 else step).start()

    send_rest(range(1, PLANE // 2))

    own = pltpu.make_async_copy(send.at[line], arrival(0, line), local_sem.at[0])
    own.start()
    plane_own = pltpu.make_async_copy(plane_send.at[0], plane_recv.at[spot], local_sem.at[1])
    plane_own.start()
    plane_own.wait()

    @pl.loop(1, PLANE)
    def _(step):
        plane_copy(step).wait()

    line_send[0] = jnp.sum(plane_recv[...], axis=0)

    @pl.loop(1, lines)
    def _(step):
        line_copy(step).start()

    line_own = pltpu.make_async_copy(line_send.at[0], line_recv.at[line], local_sem.at[2])
    line_own.start()

    send_rest(range(PLANE // 2, PLANE))

    own.wait()
    line_own.wait()

    @pl.loop(1, lines)
    def _(step):
        line_copy(step).wait()

    partner = line_recv[...]
    turn_of = (spot + PLANE - (partner // per) % PLANE) % PLANE
    place = (turn_of * lines + partner // (per * PLANE)) * per + partner % per
    places[0] = jnp.where(turn_of < EARLY, place, EARLY * lines * per)
    places[1] = place
    to_scalar = pltpu.make_async_copy(places, pairs, local_sem.at[3])
    to_scalar.start()
    to_scalar.wait()

    zero = jnp.zeros(early.shape[1:], jnp.float32)
    early[EARLY * lines * per] = zero.astype(early.dtype)

    def wait_for(turns):
        for turn in turns:
            @pl.loop(0 if turn else 1, lines)
            def _(step):
                block_copy(turn, step).wait_recv()

    def pair_sum(totals, turns, held, table):
        def add(row, totals):
            totals = list(totals)
            for turn in turns:
                lanes = lax.rem(spot + PLANE - turn, PLANE) * nq * per
                for j in range(per):
                    at = (turn * lines + row) * per + j
                    mine = held[at].astype(jnp.float32)
                    if held is early:
                        full[at] = (mine + mine).astype(full.dtype)
                    for q in range(nq):
                        other = held[pairs[table, row, 0, lanes + q * per + j]]
                        totals[q] = totals[q] + mine * other.astype(jnp.float32)
            return tuple(totals)

        return lax.fori_loop(0, lines, add, totals)

    wait_for(range(EARLY))
    totals = pair_sum((zero,) * nq, range(EARLY), early, 0)
    wait_for(range(EARLY, PLANE))
    totals = pair_sum(totals, range(EARLY, PLANE), full, 1)
    for turn in range(PLANE):
        @pl.loop(0 if turn else 1, lines)
        def _(step):
            block_copy(turn, step).wait_send()

    for q in range(nq):
        scaled = totals[q] * (1.0 / (n * per))
        out_ref[:, q, :half] = scaled[:rows]
        out_ref[:, q, half:] = scaled[rows:]


def solution(mesh):
    n = mesh.shape["ka"]

    def per_device(green_time, orbitals, pair_table, pair_momenta, owner_rows):
        per, norb, npts = orbitals.shape
        nq = pair_momenta.shape[0]
        rows = npts // n
        bf16, i32 = jnp.bfloat16, jnp.int32
        dma = pltpu.SemaphoreType.DMA
        out = pl.pallas_call(
            functools.partial(kernel, n),
            out_shape=jax.ShapeDtypeStruct((rows, nq, npts), jnp.float32),
            in_specs=[pl.BlockSpec(memory_space=pltpu.HBM)] * 5,
            out_specs=pl.BlockSpec(memory_space=pltpu.VMEM),
            scratch_shapes=[
                pltpu.SMEM((nq,), i32),
                pltpu.VMEM((per, norb, norb), bf16),
                pltpu.VMEM((per, norb, npts), bf16),
                pltpu.VMEM((per, n * per), i32),
                pltpu.VMEM((1, npts), i32),
                pltpu.VMEM((n, rows, LANES), jnp.float32),
                pltpu.VMEM((npts, npts), bf16),
                pltpu.VMEM((per, norb, npts), bf16),
                pltpu.VMEM((n, per, 2 * rows, npts // 2), bf16),
                pltpu.VMEM(((EARLY * n // PLANE + 1) * per, 2 * rows, npts // 2), bf16),
                pltpu.VMEM((n * per, 2 * rows, npts // 2), bf16),
                pltpu.VMEM((1, 1, LANES), i32),
                pltpu.VMEM((PLANE, 1, LANES), i32),
                pltpu.VMEM((1, 1, LANES), i32),
                pltpu.VMEM((n // PLANE, 1, LANES), i32),
                pltpu.VMEM((2, n // PLANE, 1, LANES), i32),
                pltpu.SMEM((2, n // PLANE, 1, LANES), i32),
                dma((3 + 2 * per,)),
                dma((n,)),
                dma((n,)),
                dma((PLANE,)),
                dma((PLANE,)),
                dma((n // PLANE,)),
                dma((n // PLANE,)),
                dma((4,)),
                pltpu.SemaphoreType.REGULAR,
            ],
            compiler_params=pltpu.CompilerParams(
                collective_id=0, has_side_effects=True, vmem_limit_bytes=32 * 1024 * 1024
            ),
            cost_estimate=pl.CostEstimate(
                flops=2 * per * npts * (norb * norb + npts * norb * 2),
                bytes_accessed=2 * per * norb * (norb + npts),
                transcendentals=0,
            ),
        )(
            *(
                pltpu.with_memory_space_constraint(operand, pltpu.HBM)
                for operand in (pair_momenta, green_time, orbitals, pair_table.T, owner_rows.reshape(1, npts))
            )
        )
        return out

    return jax.shard_map(
        per_device,
        mesh=mesh,
        in_specs=(P(("ta", "ka"), None, None), P("ka", None, None), P(None, "ka"), P(), P()),
        out_specs=P(("ta", "ka"), None, None),
        check_vma=False,
    )
```

```python
import functools

import jax
import jax.numpy as jnp
from jax import lax
from jax.experimental import pallas as pl
from jax.experimental.pallas import tpu as pltpu
from jax.sharding import PartitionSpec as P

MESH = pl.DeviceIdType.MESH
PLANE = 8
LANES = 128
EARLY = 6


def kernel(
    n, q_hbm, green_hbm, orb_hbm, table_hbm, owner_hbm, out_ref,
    q_ref, green, orb, table, owner, owner_columns, select, half_product, send, early, full,
    plane_send, plane_recv, line_send, line_recv, places, pairs,
    load_sem, send_sem, recv_sem, plane_send_sem, plane_recv_sem, line_send_sem, line_recv_sem, local_sem, ready_sem,
):
    me = lax.axis_index("ka")
    line, spot = me // PLANE, me % PLANE
    lines = n // PLANE
    per, norb, npts = orb.shape
    nq = q_ref.shape[0]
    rows = npts // n
    half = npts // 2

    def in_plane(step):
        return {"ka": line * PLANE + lax.rem(spot + step, PLANE)}

    def in_line(step):
        return {"ka": lax.rem(line + step, lines) * PLANE + spot}

    small = [
        pltpu.make_async_copy(source, held, load_sem.at[i])
        for i, (source, held) in enumerate(((owner_hbm, owner), (q_hbm, q_ref), (table_hbm, table)))
    ]
    loads = [
        (
            pltpu.make_async_copy(orb_hbm.at[k], orb.at[k], load_sem.at[3 + k]),
            pltpu.make_async_copy(green_hbm.at[k], green.at[k], load_sem.at[3 + per + k]),
        )
        for k in range(per)
    ]
    for load in small + [load for both in loads for load in both]:
        load.start()

    barrier = pltpu.get_barrier_semaphore()

    @pl.loop(1, lines)
    def _(step):
        pl.semaphore_signal(barrier, inc=1, device_id=in_line(lines - step), device_id_type=MESH)

    @pl.loop(1, PLANE)
    def _(step):
        pl.semaphore_signal(barrier, inc=1, device_id=in_plane(step), device_id_type=MESH)

    for load in small:
        load.wait()

    owner_columns[...] = jnp.transpose(
        jnp.broadcast_to(owner[...].astype(jnp.float32), (LANES, npts))
    ).reshape(n, rows, LANES)

    def project(first, last):
        for turn in range(first, last):
            place = lax.rem(spot + turn, PLANE)
            owners = jnp.concatenate([owner_columns[row * PLANE + place] for row in range(lines)], axis=0)
            for tile in range(npts // LANES):
                points = lax.broadcasted_iota(jnp.int32, owners.shape, 1) + tile * LANES
                select[turn * lines * rows : (turn + 1) * lines * rows, tile * LANES : (tile + 1) * LANES] = (
                    jnp.where(owners == points.astype(jnp.float32), 1.0, 0.0).astype(jnp.bfloat16)
                )
        for k in range(per):
            if first == 0:
                for load in loads[k]:
                    load.wait()
                half_product[k] = jnp.dot(
                    green[k], orb[k], preferred_element_type=jnp.float32
                ).astype(jnp.bfloat16)
            owned = lax.dot_general(
                select[first * lines * rows : last * lines * rows, :],
                orb[k],
                (((1,), (1,)), ((), ())),
                preferred_element_type=jnp.float32,
            ).astype(jnp.bfloat16)
            projected = jnp.dot(owned, half_product[k], preferred_element_type=jnp.float32)
            projected = projected.reshape((last - first) * lines, rows, npts)
            send[first * lines : last * lines, k] = jnp.concatenate(
                [projected[:, :, :half], projected[:, :, half:]], axis=1
            ).astype(jnp.bfloat16)

    project(0, 1)

    pl.semaphore_wait(barrier, lines - 1 + PLANE - 1)


    def arrival(turn, row):
        place = (turn * lines + row) * per
        return (early if turn < EARLY else full).at[pl.ds(place, per)]

    def block_copy(turn, step):
        peer = lax.rem(line + step, lines) * PLANE + lax.rem(spot + turn, PLANE)
        return pltpu.make_async_remote_copy(
            src_ref=send.at[turn * lines + lax.rem(line + step, lines)],
            dst_ref=arrival(turn, line),
            send_sem=send_sem.at[turn * lines + step],
            recv_sem=recv_sem.at[turn * lines + step],
            device_id={"ka": peer},
            device_id_type=MESH,
        )

    def plane_copy(step):
        return pltpu.make_async_remote_copy(
            src_ref=plane_send.at[0],
            dst_ref=plane_recv.at[spot],
            send_sem=plane_send_sem.at[step],
            recv_sem=plane_recv_sem.at[step],
            device_id=in_plane(step),
            device_id_type=MESH,
        )

    def line_copy(step):
        return pltpu.make_async_remote_copy(
            src_ref=line_send.at[0],
            dst_ref=line_recv.at[line],
            send_sem=line_send_sem.at[step],
            recv_sem=line_recv_sem.at[step],
            device_id=in_line(step),
            device_id_type=MESH,
        )

    @pl.loop(1, lines)
    def _(step):
        block_copy(0, step).start()

    @pl.loop(1, lines)
    def _(step):
        pl.semaphore_signal(ready_sem, inc=1, device_id=in_line(lines - step), device_id_type=MESH)

    table_columns = lax.broadcasted_iota(jnp.int32, table.shape, 1)
    lane = lax.broadcasted_iota(jnp.int32, (per, LANES), 1)
    which = lax.broadcasted_iota(jnp.int32, (per, LANES), 0)
    placed = jnp.zeros((per, LANES), jnp.int32)
    for q in range(nq):
        chosen = jnp.where(table_columns == q_ref[q], table[...], 0)
        partner = jnp.sum(chosen, axis=1, keepdims=True)
        placed += jnp.where(lane == (spot * nq + q) * per + which, partner, 0)
    plane_send[0] = jnp.sum(placed, axis=0, keepdims=True)

    for turn in range(1, PLANE):
        plane_copy(turn).start()

    project(1, PLANE // 2)
    for turn in range(1, PLANE // 2):
        block_copy(turn, 0).start()
    pl.semaphore_wait(ready_sem, lines - 1)

    def send_rest(turns):
        for turn in turns:
            @pl.loop(1, lines)
            def _(step):
                block_copy(turn, lines - step if turn % 2 else step).start()

    send_rest(range(1, PLANE // 2))
    project(PLANE // 2, PLANE)
    for turn in range(PLANE // 2, PLANE):
        block_copy(turn, 0).start()

    own = pltpu.make_async_copy(send.at[line], arrival(0, line), local_sem.at[0])
    own.start()
    plane_own = pltpu.make_async_copy(plane_send.at[0], plane_recv.at[spot], local_sem.at[1])
    plane_own.start()
    plane_own.wait()

    @pl.loop(1, PLANE)
    def _(step):
        plane_copy(step).wait()

    line_send[0] = jnp.sum(plane_recv[...], axis=0)

    @pl.loop(1, lines)
    def _(step):
        line_copy(step).start()

    line_own = pltpu.make_async_copy(line_send.at[0], line_recv.at[line], local_sem.at[2])
    line_own.start()

    send_rest(range(PLANE // 2, PLANE))

    own.wait()
    line_own.wait()

    @pl.loop(1, lines)
    def _(step):
        line_copy(step).wait()

    partner = line_recv[...]
    turn_of = (spot + PLANE - (partner // per) % PLANE) % PLANE
    place = (turn_of * lines + partner // (per * PLANE)) * per + partner % per
    places[0] = jnp.where(turn_of < EARLY, place, EARLY * lines * per)
    places[1] = place
    to_scalar = pltpu.make_async_copy(places, pairs, local_sem.at[3])
    to_scalar.start()
    to_scalar.wait()

    zero = jnp.zeros(early.shape[1:], jnp.float32)
    early[EARLY * lines * per] = zero.astype(early.dtype)

    def wait_for(turns):
        for turn in turns:
            @pl.loop(0 if turn else 1, lines)
            def _(step):
                block_copy(turn, step).wait()

    def pair_sum(totals, turns, held, table):
        def add(row, totals):
            totals = list(totals)
            for turn in turns:
                lanes = lax.rem(spot + PLANE - turn, PLANE) * nq * per
                for j in range(per):
                    at = (turn * lines + row) * per + j
                    mine = held[at].astype(jnp.float32)
                    if held is early:
                        full[at] = (mine + mine).astype(full.dtype)
                    for q in range(nq):
                        other = held[pairs[table, row, 0, lanes + q * per + j]]
                        totals[q] = totals[q] + mine * other.astype(jnp.float32)
            return tuple(totals)

        return lax.fori_loop(0, lines, add, totals)

    wait_for(range(EARLY))
    totals = pair_sum((zero,) * nq, range(EARLY), early, 0)
    wait_for(range(EARLY, PLANE))
    totals = pair_sum(totals, range(EARLY, PLANE), full, 1)
    for q in range(nq):
        scaled = totals[q] * (1.0 / (n * per))
        out_ref[:, q, :half] = scaled[:rows]
        out_ref[:, q, half:] = scaled[rows:]


def solution(mesh):
    n = mesh.shape["ka"]

    def per_device(green_time, orbitals, pair_table, pair_momenta, owner_rows):
        per, norb, npts = orbitals.shape
        nq = pair_momenta.shape[0]
        rows = npts // n
        bf16, i32 = jnp.bfloat16, jnp.int32
        dma = pltpu.SemaphoreType.DMA
        out = pl.pallas_call(
            functools.partial(kernel, n),
            out_shape=jax.ShapeDtypeStruct((rows, nq, npts), jnp.float32),
            in_specs=[pl.BlockSpec(memory_space=pltpu.HBM)] * 5,
            out_specs=pl.BlockSpec(memory_space=pltpu.VMEM),
            scratch_shapes=[
                pltpu.SMEM((nq,), i32),
                pltpu.VMEM((per, norb, norb), bf16),
                pltpu.VMEM((per, norb, npts), bf16),
                pltpu.VMEM((per, n * per), i32),
                pltpu.VMEM((1, npts), i32),
                pltpu.VMEM((n, rows, LANES), jnp.float32),
                pltpu.VMEM((npts, npts), bf16),
                pltpu.VMEM((per, norb, npts), bf16),
                pltpu.VMEM((n, per, 2 * rows, npts // 2), bf16),
                pltpu.VMEM(((EARLY * n // PLANE + 1) * per, 2 * rows, npts // 2), bf16),
                pltpu.VMEM((n * per, 2 * rows, npts // 2), bf16),
                pltpu.VMEM((1, 1, LANES), i32),
                pltpu.VMEM((PLANE, 1, LANES), i32),
                pltpu.VMEM((1, 1, LANES), i32),
                pltpu.VMEM((n // PLANE, 1, LANES), i32),
                pltpu.VMEM((2, n // PLANE, 1, LANES), i32),
                pltpu.SMEM((2, n // PLANE, 1, LANES), i32),
                dma((3 + 2 * per,)),
                dma((n,)),
                dma((n,)),
                dma((PLANE,)),
                dma((PLANE,)),
                dma((n // PLANE,)),
                dma((n // PLANE,)),
                dma((4,)),
                pltpu.SemaphoreType.REGULAR,
            ],
            compiler_params=pltpu.CompilerParams(
                collective_id=0, has_side_effects=True, vmem_limit_bytes=32 * 1024 * 1024
            ),
            cost_estimate=pl.CostEstimate(
                flops=2 * per * npts * (norb * norb + npts * norb * 2),
                bytes_accessed=2 * per * norb * (norb + npts),
                transcendentals=0,
            ),
        )(
            *(
                pltpu.with_memory_space_constraint(operand, pltpu.HBM)
                for operand in (pair_momenta, green_time, orbitals, pair_table.T, owner_rows.reshape(1, npts))
            )
        )
        return out

    return jax.shard_map(
        per_device,
        mesh=mesh,
        in_specs=(P(("ta", "ka"), None, None), P("ka", None, None), P(None, "ka"), P(), P()),
        out_specs=P(("ta", "ka"), None, None),
        check_vma=False,
    )
```
